128 devices in a mesh: band: 4 (over z_lo, core), space: 32 (over x, y, z_hi).
Axes of the slice: x: 4, y: 4, z: 4 (z_hi: 2, z_lo: 2; z = z_hi * 2 + z_lo), core: 2. Of those that a mesh axis runs over, the one named last changes fastest.
Arguments:
- orbitals: float32 [16, 384, 32, 128], P('band', 'space'), may hold values from -8.5 to 8.5
- potential: float32 [384, 32, 128], P('space'), may hold values from 0 to 0.6
- rotation: float32 [16, 16], replicated, may hold values from -1.5 to 1.5
Outputs:
- rotated: float32 [16, 384, 32, 128], P('band', 'space')
The draws below stay inside these ranges and needn't reach their ends.
All inputs are finite; a program needn't handle non-finite values.
Results may differ from the reference program's by a relative error of at most 0.00024.
Values sent between devices are 32-bit elements; how exact they have to be, the bound alone decides.
No kernel may reach another device: no remote copies, remote signals or barrier semaphores. Data moves between devices by JAX's collectives and lax.ppermute only.
A program may use at most 192 MiB of HBM per device.

```python
import math
import jax
import jax.numpy as jnp
from jax import lax

NY = 32
NZ = 128
DEGREE = 8
RADIUS = 6
ORBITALS = 16
NX = 384


def draw_orbitals(key, part):
    key = jax.random.fold_in(key, 7)
    key_rough, key_level, key_sign = jax.random.split(key, 3)
    full_shape = (ORBITALS, NX, NY, NZ)
    coords = jnp.arange(NX, dtype=jnp.float32) * (2.0 * math.pi / NX)
    profile = (1.0 + 0.5 * jnp.cos(coords)).reshape(1, NX, 1, 1)
    rough_part = jnp.clip(jax.random.normal(key_rough, full_shape, jnp.float32), -6.0, 6.0)
    magnitude = jax.random.uniform(key_level, (ORBITALS, 1, 1, 1), jnp.float32, 0.5, 1.5)
    levels = jnp.where(jax.random.bernoulli(key_sign, 0.5, (ORBITALS, 1, 1, 1)), magnitude, -magnitude)
    return rough_part + levels * profile


def level_of(key, dims, shards, smallest, high):
    def one(axis_at, shards_of):
        draws = jax.random.uniform(jax.random.fold_in(jax.random.fold_in(key, 6), axis_at), (shards_of,), jnp.float32, smallest / len(shards), high / len(shards))
        return jnp.repeat(jnp.exp(draws), dims[axis_at] // shards_of).reshape((-1,) + (1,) * (len(dims) - axis_at - 1))

    factor_of = one(*shards[0])
    for cut in shards[1:]:
        factor_of = factor_of * one(*cut)
    return factor_of


def scatter_about(key, dims, spread, bound, kind=jnp.bfloat16):
    result = spread * jax.random.normal(key, dims, jnp.float32)
    return jnp.clip(result, min=-bound, max=bound).astype(kind)


def setup_inputs(seed: int = 0) -> dict:
    seeds = jax.random.split(jax.random.key(seed), 4)
    orbitals = draw_orbitals(jax.random.fold_in(seeds[3], 71), 0)
    potential = jnp.clip(0.6 * jax.random.uniform(seeds[1], (NX, NY, NZ), jnp.float32) ** level_of(seeds[1], (NX, NY, NZ), ((0, 32),), -0.2, 0.2), 0.0, 0.6)
    rotation = scatter_about(seeds[2], (ORBITALS, ORBITALS), ORBITALS ** -0.5, 1.5, jnp.float32)
    return {"orbitals": orbitals, "potential": potential, "rotation": rotation}


COEFS = (-5369.0 / 1800.0, 12.0 / 7.0, -15.0 / 56.0, 10.0 / 189.0, -1.0 / 112.0, 2.0 / 1925.0, -1.0 / 16632.0)
CENTER = 6.75
HALF_WIDTH = 6.25


def scaled_op(field, potential):
    lap = (3.0 * COEFS[0]) * field
    for step in range(1, RADIUS + 1):
        near = jnp.roll(field, step, 0) + jnp.roll(field, -step, 0)
        near = near + jnp.roll(field, step, 1) + jnp.roll(field, -step, 1)
        near = near + jnp.roll(field, step, 2) + jnp.roll(field, -step, 2)
        lap = lap + COEFS[step] * near
    applied = -0.5 * lap + potential * field
    return (applied - CENTER * field) / HALF_WIDTH


def reference(orbitals, potential, rotation):
    def filter_one(field):
        previous = field
        current = scaled_op(field, potential)
        for step in range(1, DEGREE):
            following = 2.0 * scaled_op(current, potential) - previous
            previous = current
            current = following
        return current

    filtered = lax.map(filter_one, orbitals)
    return jnp.tensordot(rotation, filtered, axes=((0,), (0,)), precision=lax.Precision.HIGHEST)
```

```python
import jax
import jax.numpy as jnp
import ml_dtypes
import numpy as np
from jax import lax
from jax.experimental import pallas as pl
from jax.experimental.pallas import tpu as pltpu
from jax.sharding import PartitionSpec as P


NY, NZ = 32, 128
DEGREE = 8
RADIUS = 6
SLAB = 12
HALF = 6
SEG = 48
COEFS = (
    -5369.0 / 1800.0,
    12.0 / 7.0,
    -15.0 / 56.0,
    10.0 / 189.0,
    -1.0 / 112.0,
    2.0 / 1925.0,
    -1.0 / 16632.0,
)
CENTER = 6.75
HALF_WIDTH = 6.25
GAINS = tuple(-c / HALF_WIDTH for c in COEFS)
POT_SCALE = 2.0 / HALF_WIDTH
BF16, F32 = jnp.bfloat16, jnp.float32
AXES = ("band", "space")
VMEM_LIMIT = 48 * 1024 * 1024


def split_gain(j):
    high = np.float32(GAINS[j]).astype(ml_dtypes.bfloat16)
    low = np.float32(GAINS[j] - float(high)).astype(ml_dtypes.bfloat16)
    return high, low


def circulant(n):
    high = np.zeros((n, n), ml_dtypes.bfloat16)
    low = np.zeros((n, n), ml_dtypes.bfloat16)
    for j in range(1, RADIUS + 1):
        for i in range(n):
            for k in ((i + j) % n, (i - j) % n):
                high[i, k], low[i, k] = split_gain(j)
    return high, low


GAIN_GAP = 4.0 * sum(
    GAINS[j] - float(split_gain(j)[0]) - float(split_gain(j)[1]) for j in range(1, RADIUS + 1)
)
POT_SHIFT = (-2.0 * CENTER - 3.0 * COEFS[0]) / HALF_WIDTH + GAIN_GAP


def z_matrix():
    high, low = circulant(NZ)
    return np.block([[high, low], [high, np.zeros_like(low)]])


def y_matrix():
    high, low = circulant(NY)
    return np.concatenate([high, high, low], axis=1)


def index_of(x, y, z, core):
    return ((z % 2) * 2 + core) * 32 + (x % 4) * 8 + y * 2 + z // 2


DEVICES = [(x, y, z, c) for x in range(4) for y in range(4) for z in range(4) for c in range(2)]


def permute(array, target):
    pairs = []
    for device in DEVICES:
        to = target(*device)
        if to is not None:
            pairs.append((index_of(*device), index_of(*to)))
    return lax.ppermute(array, AXES, pairs)


def other_core(x, y, z, core):
    return (x, y, z, 1 - core)


def x_neighbour(x, y, z, core):
    return (x - 1, y, z, 1) if core == 0 else (x + 1, y, z, 0)


def host_of(which, core):
    lo, i = which >> 2, which & 3
    return core * 2 + (i >> 1), 2 * (i & 1) + 1 - lo


def place():
    band, space = lax.axis_index("band"), lax.axis_index("space")
    return band // 2, band % 2, (space // 2) % 4, space % 2


def mix_kernel(rotation, keep, got, keep_other, got_other, out):
    lo, core, y, hi = place()
    flip = (y % 2) * 4 + hi * 2 + lo
    groups = (
        (keep, lo, core),
        (got, 1 - lo, core),
        (keep_other, lo, 1 - core),
        (got_other, 1 - lo, 1 - core),
    )
    for r in range(8):
        which = r ^ flip
        column = 4 * (2 * (which >> 2) + core) + (which & 3)
        total = None
        for ref, lo_from, core_from in groups:
            for i in range(4):
                term = rotation[4 * (2 * lo_from + core_from) + i, column] * ref[i]
                total = term if total is None else total + term
        out[r] = total


def block(a, b, w, w_at, zmat, ymat, at, first):
    n = SLAB
    u = a[at : at + n]
    high = u.astype(BF16)
    low = (u - high.astype(F32)).astype(BF16)
    both = jnp.concatenate([high.reshape(n * NY, NZ), low.reshape(n * NY, NZ)], axis=1)
    zz = jnp.dot(both, zmat[...], preferred_element_type=F32)
    z = (zz[:, :NZ] + zz[:, NZ:]).reshape(n, NY, NZ)
    ys = []
    for i in range(0, n, 2):
        rows = [jnp.concatenate([q[i], q[i + 1]], axis=1) for q in (high, low, high)]
        pair = jnp.dot(ymat[...], jnp.concatenate(rows, axis=0), preferred_element_type=F32)
        ys += [pair[:, :NZ], pair[:, NZ:]]
    for r in range(0, NY, 8):
        x = a[at - RADIUS : at + n + RADIUS, r : r + 8]
        total = w[at - w_at : at - w_at + n, r : r + 8] * x[RADIUS : RADIUS + n] + z[:, r : r + 8]
        total = total + jnp.stack([t[r : r + 8] for t in ys])
        for j in range(1, RADIUS + 1):
            near = x[RADIUS + j : RADIUS + j + n] + x[RADIUS - j : RADIUS - j + n]
            total = total + GAINS[j] * near
        if first:
            b[at : at + n, r : r + 8] = 0.5 * total
        else:
            b[at : at + n, r : r + 8] = total - b[at : at + n, r : r + 8]


KEPT = SEG - RADIUS


def lay_segment(ref, to, at, core, which):
    for s in range(8):
        source = jnp.where(core == 1, s, 7 - s) ^ which
        for t in range(HALF):
            to[at + HALF * s + t] = ref[source, jnp.where(core == 1, t, HALF - 1 - t)]


def first_kernel(own, other, pot, pot_other, zmat, ymat, even_out, odd_out, w_out, even, odd, w):
    lo, core, y, hi = place()
    which = (1 - lo) * 4 + (y % 2) * 2 + hi
    lay_segment(other, even, 0, core, which)
    lay_segment(own, even, SEG, core, which)
    for s in range(8):
        ref = pot if s % 2 else pot_other
        d = jnp.where(core == 1, s >> 1, 3 - (s >> 1)) ^ y
        for t in range(SLAB):
            plane = ref[d, jnp.where(core == 1, t, SLAB - 1 - t)]
            w[SLAB * s + t] = plane * POT_SCALE + POT_SHIFT
    for k in range(1, DEGREE):
        a, b = (even, odd) if k % 2 else (odd, even)
        for at in range(RADIUS * k, 2 * SEG - RADIUS * k, SLAB):
            block(a, b, w, 0, zmat, ymat, at, k == 1)
    even_out[...] = even[KEPT:]
    odd_out[...] = odd[KEPT:]
    w_out[...] = w[SEG:]


def second_kernel(even_in, odd_in, w_in, halo, pot, zmat, ymat, out, even, odd, w):
    lo, core, y, hi = place()
    which = (1 - lo) * 4 + (y % 2) * 2 + hi
    shift = KEPT
    even[0 : 2 * SEG - shift] = even_in[...]
    odd[0 : 2 * SEG - shift] = odd_in[...]
    w[0:SEG] = w_in[...]
    lay_segment(halo, even, 2 * SEG - shift, core, which)
    for s in range(4):
        d = (jnp.where(core == 1, s >> 1, 3 - (s >> 1)) ^ y) & 1
        for t in range(SLAB):
            plane = pot[s & 1, d, jnp.where(core == 1, t, SLAB - 1 - t)]
            w[SEG + SLAB * s + t] = plane * POT_SCALE + POT_SHIFT
    for k in range(1, DEGREE + 1):
        a, b = (even, odd) if k % 2 else (odd, even)
        for at in range(2 * SEG - RADIUS * k, 3 * SEG - RADIUS * k, SLAB):
            block(a, b, w, SEG - shift, zmat, ymat, at - shift, k == 1)
    mine = (y % 2) * 2 + hi
    for s in range(4):
        slot = jnp.where(core == 1, s, 3 - s) ^ mine
        for t in range(SLAB):
            plane = even[SEG - shift + SLAB * s + t]
            out[slot, jnp.where(core == 1, t, SLAB - 1 - t)] = plane


def planes(*lead):
    return jax.ShapeDtypeStruct((*lead, NY, NZ), F32)


def vmem(n):
    return [pl.BlockSpec(memory_space=pltpu.VMEM)] * n


def call(kernel, outs, scratch, flops, *operands, scalars=0):
    specs = [pl.BlockSpec(memory_space=pltpu.SMEM)] * scalars + vmem(len(operands) - scalars)
    moved = 4 * sum(x.size for x in (*operands, *outs))
    return pl.pallas_call(
        kernel,
        out_shape=outs,
        in_specs=specs,
        out_specs=vmem(len(outs)),
        scratch_shapes=[pltpu.VMEM((n, NY, NZ), F32) for n in scratch],
        compiler_params=pltpu.CompilerParams(vmem_limit_bytes=VMEM_LIMIT),
        cost_estimate=pl.CostEstimate(flops=flops, bytes_accessed=moved, transcendentals=0),
    )(*operands)


def gather_potential(potential, core, y, hi):
    far = permute(potential, lambda x, y, z, c: (x, y, 3 - z, c) if c == z // 2 else None)
    mine = jnp.where(core == hi, potential, far)
    parts = [mine]
    for d in range(1, 4):
        parts.append(permute(mine, lambda x, y, z, c: (x, y ^ d, z, c)))
    here = jnp.stack(parts)
    there = permute(here, other_core)
    start = 2 * ((y // 2) ^ core)
    both = jnp.stack([lax.dynamic_slice_in_dim(v, start, 2, 0) for v in (here, there)])
    return here, there, permute(both, x_neighbour)


def local(orbitals, potential, rotation):
    lo, core, y, hi = place()
    here, there, beyond = gather_potential(potential, core, y, hi)

    keep = lax.dynamic_slice_in_dim(orbitals, HALF * lo, HALF, 1)
    give = lax.dynamic_slice_in_dim(orbitals, HALF * (1 - lo), HALF, 1)
    got = permute(give, lambda x, y, z, c: (x, y, z ^ 1, c))
    keep_other = permute(keep, other_core)
    got_other = permute(got, other_core)
    (mixed,) = call(
        mix_kernel, [planes(8, HALF)], [], 1 << 22, rotation, keep, got, keep_other, got_other, scalars=1
    )

    pieces = []
    for r in range(8):

        def to_host(x, y, z, c):
            which = r ^ ((y % 2) * 4 + (z // 2) * 2 + z % 2)
            return (x, *host_of(which, c), y // 2)

        pieces.append(permute(mixed[r], to_host))
    own = jnp.stack(pieces)
    other = permute(own, other_core)
    halo = permute(own, x_neighbour)

    zmat, ymat = jnp.asarray(z_matrix()), jnp.asarray(y_matrix())
    kept = 2 * SEG - KEPT
    even, odd, w = call(
        first_kernel,
        [planes(kept), planes(kept), planes(SEG)],
        [2 * SEG, 2 * SEG, 2 * SEG],
        1 << 29,
        own,
        other,
        here,
        there,
        zmat,
        ymat,
    )
    (filtered,) = call(
        second_kernel,
        [planes(4, SLAB)],
        [3 * SEG - KEPT, 3 * SEG - KEPT, 2 * SEG],
        1 << 29,
        even,
        odd,
        w,
        halo,
        beyond,
        zmat,
        ymat,
    )

    result = jnp.zeros(orbitals.shape, F32)
    mine = (y % 2) * 2 + hi
    for r in range(4):

        def to_owner(x, y, z, c):
            slab = r ^ ((y % 2) * 2 + z // 2)
            return (x, 2 * c + (slab >> 1), 2 * (slab & 1) + 1 - z % 2, y // 2)

        piece = permute(filtered[r], to_owner)
        result = lax.dynamic_update_slice_in_dim(result, piece[None], r ^ mine, 0)
    return result


def solution(mesh):
    return jax.shard_map(
        local,
        mesh=mesh,
        in_specs=(P("band", "space", None, None), P("space", None, None), P()),
        out_specs=P("band", "space", None, None),
        check_vma=False,
    )
```

```python
import jax
import jax.numpy as jnp
import ml_dtypes
import numpy as np
from jax import lax
from jax.experimental import pallas as pl
from jax.experimental.pallas import tpu as pltpu
from jax.sharding import PartitionSpec as P


NY, NZ = 32, 128
DEGREE = 8
RADIUS = 6
SLAB = 12
RUN = 3
SEG = 48
COEFS = (
    -5369.0 / 1800.0,
    12.0 / 7.0,
    -15.0 / 56.0,
    10.0 / 189.0,
    -1.0 / 112.0,
    2.0 / 1925.0,
    -1.0 / 16632.0,
)
CENTER = 6.75
HALF_WIDTH = 6.25
GAINS = tuple(-c / HALF_WIDTH for c in COEFS)
POT_SCALE = 2.0 / HALF_WIDTH
BF16, F32 = jnp.bfloat16, jnp.float32
AXES = ("band", "space")
VMEM_LIMIT = 48 * 1024 * 1024


def split_gain(j):
    high = np.float32(GAINS[j]).astype(ml_dtypes.bfloat16)
    low = np.float32(GAINS[j] - float(high)).astype(ml_dtypes.bfloat16)
    return high, low


def circulant(n):
    high = np.zeros((n, n), ml_dtypes.bfloat16)
    low = np.zeros((n, n), ml_dtypes.bfloat16)
    for j in range(1, RADIUS + 1):
        for i in range(n):
            for k in ((i + j) % n, (i - j) % n):
                high[i, k], low[i, k] = split_gain(j)
    return high, low


GAIN_GAP = 4.0 * sum(
    GAINS[j] - float(split_gain(j)[0]) - float(split_gain(j)[1]) for j in range(1, RADIUS + 1)
)
POT_SHIFT = (-2.0 * CENTER - 3.0 * COEFS[0]) / HALF_WIDTH + GAIN_GAP


def z_matrix():
    high, low = circulant(NZ)
    return np.block([[high, low], [high, np.zeros_like(low)]])


def y_matrix():
    high, low = circulant(NY)
    return np.concatenate([high, high, low], axis=1)


def index_of(x, y, z, core):
    return ((z % 2) * 2 + core) * 32 + (x % 4) * 8 + y * 2 + z // 2


DEVICES = [(x, y, z, c) for x in range(4) for y in range(4) for z in range(4) for c in range(2)]


def permute(array, target):
    pairs = []
    for device in DEVICES:
        to = target(*device)
        if to is not None:
            pairs.append((index_of(*device), index_of(*to)))
    return lax.ppermute(array, AXES, pairs)


def other_core(x, y, z, core):
    return (x, y, z, 1 - core)


def x_neighbour(x, y, z, core):
    return (x - 1, y, z, 1) if core == 0 else (x + 1, y, z, 0)


def host_of(c):
    lo, core, i = c >> 3, (c >> 2) & 1, c & 3
    return core * 2 + (i >> 1), 2 * (i & 1) + 1 - lo


HOSTS = [host_of(c) for c in range(16)]


def low_slab(y, core):
    return (y // 2) ^ (y % 2) ^ core


def source_of_run(core):
    runs = [low_slab(y, core) * 8 + (z // 2) * 4 + (y // 2) * 2 + z % 2 for y, z in HOSTS]
    return [runs.index(run) for run in range(16)]


def place():
    band, space = lax.axis_index("band"), lax.axis_index("space")
    return band // 2, band % 2, (space // 2) % 4, space % 2


def mix_kernel(rotation, first, second, third, fourth, out):
    lo, core, y, hi = place()
    mine = (y // 2) * 2 + lo
    for c in range(0, 16, 2):
        totals = [None, None]
        for r, ref in enumerate((first, second, third, fourth)):
            for i in range(4):
                cells = ref[i]
                for d in range(2):
                    term = rotation[4 * (r ^ mine) + i, c + d] * cells
                    totals[d] = term if totals[d] is None else totals[d] + term
        for d in range(2):
            out[c + d] = totals[d]


def block(a, b, w, w_at, zmat, ymat, at, first):
    n = SLAB
    u = a[at : at + n]
    high = u.astype(BF16)
    low = (u - high.astype(F32)).astype(BF16)
    both = jnp.concatenate([high.reshape(n * NY, NZ), low.reshape(n * NY, NZ)], axis=1)
    zz = jnp.dot(both, zmat[...], preferred_element_type=F32)
    z = (zz[:, :NZ] + zz[:, NZ:]).reshape(n, NY, NZ)
    ys = []
    for i in range(0, n, 2):
        rows = [jnp.concatenate([q[i], q[i + 1]], axis=1) for q in (high, low, high)]
        pair = jnp.dot(ymat[...], jnp.concatenate(rows, axis=0), preferred_element_type=F32)
        ys += [pair[:, :NZ], pair[:, NZ:]]
    for r in range(0, NY, 8):
        x = a[at - RADIUS : at + n + RADIUS, r : r + 8]
        total = w[at - w_at : at - w_at + n, r : r + 8] * x[RADIUS : RADIUS + n] + z[:, r : r + 8]
        total = total + jnp.stack([t[r : r + 8] for t in ys])
        for j in range(1, RADIUS + 1):
            near = x[RADIUS + j : RADIUS + j + n] + x[RADIUS - j : RADIUS - j + n]
            total = total + GAINS[j] * near
        if first:
            b[at : at + n, r : r + 8] = 0.5 * total
        else:
            b[at : at + n, r : r + 8] = total - b[at : at + n, r : r + 8]


KEPT = SEG - RADIUS


def lay_segment(ref, to, at, core, same):
    ahead = source_of_run(1 if same else 0)
    back = source_of_run(0 if same else 1)
    for s in range(16):
        source = jnp.where(core == 1, ahead[s], back[15 - s])
        for t in range(RUN):
            to[at + RUN * s + t] = ref[source, jnp.where(core == 1, t, RUN - 1 - t)]


def lay_potential(ref, to, at, core, core_from, y, hi):
    for s in range(4):
        slab = jnp.where(core == 1, s, 3 - s)
        source = ((slab & 1) ^ hi) * 2 + ((slab >> 1) ^ low_slab(y, core_from))
        for t in range(SLAB):
            plane = ref[source, jnp.where(core == 1, t, SLAB - 1 - t)]
            to[at + SLAB * s + t] = plane * POT_SCALE + POT_SHIFT


def first_kernel(own, other, pot, pot_other, zmat, ymat, even_out, odd_out, w_out, even, odd, w):
    lo, core, y, hi = place()
    lay_segment(other, even, 0, core, False)
    lay_segment(own, even, SEG, core, True)
    lay_potential(pot_other, w, 0, core, 1 - core, y, hi)
    lay_potential(pot, w, SEG, core, core, y, hi)
    for k in range(1, DEGREE):
        a, b = (even, odd) if k % 2 else (odd, even)
        for at in range(RADIUS * k, 2 * SEG - RADIUS * k, SLAB):
            block(a, b, w, 0, zmat, ymat, at, k == 1)
    even_out[...] = even[KEPT:]
    odd_out[...] = odd[KEPT:]
    w_out[...] = w[SEG:]


def second_kernel(even_in, odd_in, w_in, halo, pot, zmat, ymat, out, even, odd, w):
    lo, core, y, hi = place()
    shift = KEPT
    even[0 : 2 * SEG - shift] = even_in[...]
    odd[0 : 2 * SEG - shift] = odd_in[...]
    w[0:SEG] = w_in[...]
    lay_segment(halo, even, 2 * SEG - shift, core, False)
    lay_potential(pot, w, SEG, core, 1 - core, y, hi)
    for k in range(1, DEGREE + 1):
        a, b = (even, odd) if k % 2 else (odd, even)
        for at in range(2 * SEG - RADIUS * k, 3 * SEG - RADIUS * k, SLAB):
            block(a, b, w, SEG - shift, zmat, ymat, at - shift, k == 1)
    mine = (y % 2) * 2 + hi
    for s in range(4):
        slot = jnp.where(core == 1, s, 3 - s) ^ mine
        for t in range(SLAB):
            plane = even[SEG - shift + SLAB * s + t]
            out[slot, jnp.where(core == 1, t, SLAB - 1 - t)] = plane


def planes(*lead):
    return jax.ShapeDtypeStruct((*lead, NY, NZ), F32)


def vmem(n):
    return [pl.BlockSpec(memory_space=pltpu.VMEM)] * n


def call(kernel, outs, scratch, flops, *operands, scalars=0):
    specs = [pl.BlockSpec(memory_space=pltpu.SMEM)] * scalars + vmem(len(operands) - scalars)
    moved = 4 * sum(x.size for x in (*operands, *outs))
    return pl.pallas_call(
        kernel,
        out_shape=outs,
        in_specs=specs,
        out_specs=vmem(len(outs)),
        scratch_shapes=[pltpu.VMEM((n, NY, NZ), F32) for n in scratch],
        compiler_params=pltpu.CompilerParams(vmem_limit_bytes=VMEM_LIMIT),
        cost_estimate=pl.CostEstimate(flops=flops, bytes_accessed=moved, transcendentals=0),
    )(*operands)


def spread_run(orbitals, band, r):
    def to_run(x, y, z, c):
        run = r ^ (2 * (z % 2) + c)
        far, core = run >> 1, y // 2
        return (x, 2 * far + ((y % 2) ^ core ^ far), 2 * (z // 2) + (run & 1), core)

    return permute(lax.dynamic_slice_in_dim(orbitals, RUN * (r ^ band), RUN, 1), to_run)


def local(orbitals, potential, rotation):
    lo, core, y, hi = place()
    groups = [spread_run(orbitals, 2 * lo + core, r) for r in range(4)]
    near = permute(potential, lambda x, y, z, c: (x, 3 - y, z, c) if c == y // 2 else None)
    near = jnp.where(core == y // 2, potential, near)
    far = permute(potential, lambda x, y, z, c: (x, y ^ 1 if c == y // 2 else y ^ 2, z, y // 2))
    pair = jnp.stack([near, far])
    next_z = permute(pair, lambda x, y, z, c: (x, y, 3 - z, c))
    pot = jnp.concatenate([pair, next_z])
    (mixed,) = call(mix_kernel, [planes(16, RUN)], [], 1 << 22, rotation, *groups, scalars=1)
    pot_halo = permute(pot, x_neighbour)
    pot_other = permute(pot, other_core)
    plane_of_hosts = [[index_of(x, *chip, c) for chip in HOSTS] for x in range(4) for c in range(2)]
    own = lax.all_to_all(mixed, AXES, 0, 0, tiled=True, axis_index_groups=plane_of_hosts)
    own, pot_halo, pot_other = lax.optimization_barrier((own, pot_halo, pot_other))
    other = permute(own, other_core)
    halo = permute(own, x_neighbour)

    zmat, ymat = jnp.asarray(z_matrix()), jnp.asarray(y_matrix())
    kept = 2 * SEG - KEPT
    even, odd, w = call(
        first_kernel,
        [planes(kept), planes(kept), planes(SEG)],
        [2 * SEG, 2 * SEG, 2 * SEG],
        1 << 29,
        own,
        other,
        pot,
        pot_other,
        zmat,
        ymat,
    )
    (filtered,) = call(
        second_kernel,
        [planes(4, SLAB)],
        [3 * SEG - KEPT, 3 * SEG - KEPT, 2 * SEG],
        1 << 29,
        even,
        odd,
        w,
        halo,
        pot_halo,
        zmat,
        ymat,
    )

    result = jnp.zeros(orbitals.shape, F32)
    mine = (y % 2) * 2 + hi
    for r in range(4):

        def to_owner(x, y, z, c):
            slab = r ^ ((y % 2) * 2 + z // 2)
            return (x, 2 * c + (slab >> 1), 2 * (slab & 1) + 1 - z % 2, y // 2)

        piece = permute(filtered[r], to_owner)
        result = lax.dynamic_update_slice_in_dim(result, piece[None], r ^ mine, 0)
    return result


def solution(mesh):
    return jax.shard_map(
        local,
        mesh=mesh,
        in_specs=(P("band", "space", None, None), P("space", None, None), P()),
        out_specs=P("band", "space", None, None),
        check_vma=False,
    )
```

```python
import jax
import jax.numpy as jnp
import ml_dtypes
import numpy as np
from jax import lax
from jax.experimental import pallas as pl
from jax.experimental.pallas import tpu as pltpu
from jax.sharding import PartitionSpec as P


NY, NZ = 32, 128
DEGREE = 8
RADIUS = 6
SLAB = 12
RUN = 3
SEG = 48
COEFS = (
    -5369.0 / 1800.0,
    12.0 / 7.0,
    -15.0 / 56.0,
    10.0 / 189.0,
    -1.0 / 112.0,
    2.0 / 1925.0,
    -1.0 / 16632.0,
)
CENTER = 6.75
HALF_WIDTH = 6.25
GAINS = tuple(-c / HALF_WIDTH for c in COEFS)
POT_SCALE = 2.0 / HALF_WIDTH
BF16, F32 = jnp.bfloat16, jnp.float32
AXES = ("band", "space")
VMEM_LIMIT = 16 * 1024 * 1024


def split_gain(j):
    high = np.float32(GAINS[j]).astype(ml_dtypes.bfloat16)
    low = np.float32(GAINS[j] - float(high)).astype(ml_dtypes.bfloat16)
    return high, low


def circulant(n):
    high = np.zeros((n, n), ml_dtypes.bfloat16)
    low = np.zeros((n, n), ml_dtypes.bfloat16)
    for j in range(1, RADIUS + 1):
        for i in range(n):
            for k in ((i + j) % n, (i - j) % n):
                high[i, k], low[i, k] = split_gain(j)
    return high, low


GAIN_GAP = 4.0 * sum(
    GAINS[j] - float(split_gain(j)[0]) - float(split_gain(j)[1]) for j in range(1, RADIUS + 1)
)
POT_SHIFT = (-2.0 * CENTER - 3.0 * COEFS[0]) / HALF_WIDTH + GAIN_GAP


def z_matrix():
    high, low = circulant(NZ)
    return np.block([[high, low], [high, np.zeros_like(low)]])


def y_matrix():
    high, low = circulant(NY)
    return np.concatenate([high, high, low], axis=1)


def index_of(x, y, z, core):
    return ((z % 2) * 2 + core) * 32 + (x % 4) * 8 + y * 2 + z // 2


DEVICES = [(x, y, z, c) for x in range(4) for y in range(4) for z in range(4) for c in range(2)]


def permute(array, target):
    pairs = []
    for device in DEVICES:
        to = target(*device)
        if to is not None:
            pairs.append((index_of(*device), index_of(*to)))
    return lax.ppermute(array, AXES, pairs)


def other_core(x, y, z, core):
    return (x, y, z, 1 - core)


def x_neighbour(x, y, z, core):
    return (x - 1, y, z, 1) if core == 0 else (x + 1, y, z, 0)


def host_of(c):
    lo, core, i = c >> 3, (c >> 2) & 1, c & 3
    return core * 2 + (i >> 1), 2 * (i & 1) + 1 - lo


HOSTS = [host_of(c) for c in range(16)]


def low_slab(y, core):
    return (y // 2) ^ (y % 2) ^ core


def source_of_run(core):
    runs = [low_slab(y, core) * 8 + (z // 2) * 4 + (y // 2) * 2 + z % 2 for y, z in HOSTS]
    return [runs.index(run) for run in range(16)]


HALVES = [[j for j, (y, z) in enumerate(HOSTS) if low_slab(y, 0) == far] for far in range(2)]


def place():
    band, space = lax.axis_index("band"), lax.axis_index("space")
    return band // 2, band % 2, (space // 2) % 4, space % 2


def mix_kernel(rotation, first, second, third, fourth, out):
    lo, core, y, hi = place()
    for c in range(0, 16, 2):
        totals = [None, None]
        for r, ref in enumerate((first, second, third, fourth)):
            band = 2 * (lo ^ (r & 1)) + ((r >> 1) ^ (y // 2) ^ core)
            for i in range(4):
                cells = ref[i]
                for d in range(2):
                    term = rotation[4 * band + i, c + d] * cells
                    totals[d] = term if totals[d] is None else totals[d] + term
        for d in range(2):
            out[c + d] = totals[d]


def block(a, b, w, w_at, zmat, ymat, at, first):
    n = SLAB
    u = a[at : at + n]
    high = u.astype(BF16)
    low = (u - high.astype(F32)).astype(BF16)
    both = jnp.concatenate([high.reshape(n * NY, NZ), low.reshape(n * NY, NZ)], axis=1)
    zz = jnp.dot(both, zmat[...], preferred_element_type=F32)
    z = (zz[:, :NZ] + zz[:, NZ:]).reshape(n, NY, NZ)
    ys = []
    for i in range(0, n, 2):
        rows = [jnp.concatenate([q[i], q[i + 1]], axis=1) for q in (high, low, high)]
        pair = jnp.dot(ymat[...], jnp.concatenate(rows, axis=0), preferred_element_type=F32)
        ys += [pair[:, :NZ], pair[:, NZ:]]
    for r in range(0, NY, 8):
        x = a[at - RADIUS : at + n + RADIUS, r : r + 8]
        total = w[at - w_at : at - w_at + n, r : r + 8] * x[RADIUS : RADIUS + n] + z[:, r : r + 8]
        total = total + jnp.stack([t[r : r + 8] for t in ys])
        for j in range(1, RADIUS + 1):
            near = x[RADIUS + j : RADIUS + j + n] + x[RADIUS - j : RADIUS - j + n]
            total = total + GAINS[j] * near
        if first:
            b[at : at + n, r : r + 8] = 0.5 * total
        else:
            b[at : at + n, r : r + 8] = total - b[at : at + n, r : r + 8]


KEPT = SEG - RADIUS


def lay_segment(ref, to, at, core, same):
    ahead = source_of_run(1 if same else 0)
    back = source_of_run(0 if same else 1)
    for s in range(16):
        source = jnp.where(core == 1, ahead[s], back[15 - s])
        for t in range(RUN):
            to[at + RUN * s + t] = ref[source, jnp.where(core == 1, t, RUN - 1 - t)]


def lay_potential(ref, to, at, core, core_from, y, hi, slabs=4):
    for s in range(slabs):
        slab = jnp.where(core == 1, s, 3 - s)
        source = ((slab & 1) ^ hi) * 2 + ((slab >> 1) ^ low_slab(y, core_from))
        for t in range(SLAB):
            plane = ref[source, jnp.where(core == 1, t, SLAB - 1 - t)]
            to[at + SLAB * s + t] = plane * POT_SCALE + POT_SHIFT


def first_kernel(own, other, pot, pot_other, zmat, ymat, even_out, odd_out, w_out, even, odd, w):
    lo, core, y, hi = place()
    lay_segment(other, even, 0, core, False)
    lay_segment(own, even, SEG, core, True)
    lay_potential(pot_other, w, 0, core, 1 - core, y, hi)
    lay_potential(pot, w, SEG, core, core, y, hi)
    for k in range(1, DEGREE):
        a, b = (even, odd) if k % 2 else (odd, even)
        for at in range(RADIUS * k, 2 * SEG - RADIUS * k, SLAB):
            block(a, b, w, 0, zmat, ymat, at, k == 1)
    even_out[...] = even[KEPT:]
    odd_out[...] = odd[KEPT:]
    w_out[...] = w[SEG:]


def lay_half(ref, to, at, core, half):
    ahead, back = source_of_run(0), source_of_run(1)
    for s in range(8):
        slots = [HALVES[half].index(table) for table in (ahead[8 * half + s], back[15 - 8 * half - s])]
        source = jnp.where(core == 1, *slots)
        for t in range(RUN):
            to[at + RUN * s + t] = ref[source, jnp.where(core == 1, t, RUN - 1 - t)]


NEAR = 3 * SEG - SEG // 2


def second_kernel(even_in, odd_in, w_in, halo, pot, zmat, ymat, even_out, odd_out, even, odd, w):
    lo, core, y, hi = place()
    shift = KEPT
    even[0 : 2 * SEG - shift] = even_in[...]
    odd[0 : 2 * SEG - shift] = odd_in[...]
    w[0:SEG] = w_in[...]
    lay_half(halo, even, 2 * SEG - shift, core, 0)
    lay_potential(pot, w, SEG, core, 1 - core, y, hi, 2)
    for k in range(1, DEGREE + 1):
        a, b = (even, odd) if k % 2 else (odd, even)
        for at in range(2 * SEG - RADIUS * k, NEAR - RADIUS * k, SLAB):
            block(a, b, w, SEG - shift, zmat, ymat, at - shift, k == 1)
    even_out[...] = even[RADIUS:]
    odd_out[...] = odd[RADIUS:]


def third_kernel(even_in, odd_in, w_in, halo, pot, zmat, ymat, out, even, odd, w):
    lo, core, y, hi = place()
    shift = SEG
    even[0 : NEAR - shift] = even_in[...]
    odd[0 : NEAR - shift] = odd_in[...]
    w[SEG // 2 : SEG] = w_in[SEG // 2 :]
    lay_half(halo, even, NEAR - shift, core, 1)
    lay_potential(pot, w, SEG, core, 1 - core, y, hi)
    for k in range(1, DEGREE + 1):
        a, b = (even, odd) if k % 2 else (odd, even)
        for at in range(NEAR - RADIUS * k, 3 * SEG - RADIUS * k, SLAB):
            block(a, b, w, SEG - shift, zmat, ymat, at - shift, k == 1)
    mine = ((y % 2) ^ (y // 2) ^ core) * 2 + hi
    for s in range(4):
        slot = jnp.where(core == 1, s, 3 - s) ^ mine
        for t in range(SLAB):
            plane = even[SEG - shift + SLAB * s + t]
            out[slot, jnp.where(core == 1, t, SLAB - 1 - t)] = plane


def planes(*lead):
    return jax.ShapeDtypeStruct((*lead, NY, NZ), F32)


def vmem(n):
    return [pl.BlockSpec(memory_space=pltpu.VMEM)] * n


def call(kernel, outs, scratch, flops, *operands, scalars=0):
    specs = [pl.BlockSpec(memory_space=pltpu.SMEM)] * scalars + vmem(len(operands) - scalars)
    moved = 4 * sum(x.size for x in (*operands, *outs))
    return pl.pallas_call(
        kernel,
        out_shape=outs,
        in_specs=specs,
        out_specs=vmem(len(outs)),
        scratch_shapes=[pltpu.VMEM((n, NY, NZ), F32) for n in scratch],
        compiler_params=pltpu.CompilerParams(vmem_limit_bytes=VMEM_LIMIT),
        cost_estimate=pl.CostEstimate(flops=flops, bytes_accessed=moved, transcendentals=0),
    )(*operands)


def spread_run(cells, r):
    def to_run(x, y, z, c):
        far, core = (r >> 1) ^ c ^ (y // 2), y // 2
        return (x, y if far == core else 3 - y, z ^ (r & 1), core)

    return permute(cells, to_run)


def local(orbitals, potential, rotation):
    lo, core, y, hi = place()
    runs = [2 * ((r >> 1) ^ core ^ (y // 2)) + (lo ^ (r & 1)) for r in range(4)]
    cells = [lax.dynamic_slice_in_dim(orbitals, RUN * run, RUN, 1) for run in runs]
    near = permute(potential, lambda x, y, z, c: (x, 3 - y, z, c) if c == y // 2 else None)
    far = permute(potential, lambda x, y, z, c: (x, y ^ 1 if c == y // 2 else y ^ 2, z, y // 2))
    near, *cells = lax.optimization_barrier((near, *cells))
    near = jnp.where(core == y // 2, potential, near)
    pair = jnp.stack([near, far])
    next_z = permute(pair, lambda x, y, z, c: (x, y, 3 - z, c))
    pot = jnp.concatenate([pair, next_z])
    groups = [spread_run(part, r) for r, part in enumerate(cells)]
    (mixed,) = call(mix_kernel, [planes(16, RUN)], [], 1 << 22, rotation, *groups, scalars=1)
    pot_halo = permute(pot, x_neighbour)
    pot_other = permute(pot, other_core)
    plane_of_hosts = [[index_of(x, *chip, c) for chip in HOSTS] for x in range(4) for c in range(2)]
    own = lax.all_to_all(mixed, AXES, 0, 0, tiled=True, axis_index_groups=plane_of_hosts)
    own, pot_halo, pot_other = lax.optimization_barrier((own, pot_halo, pot_other))
    other = permute(own, other_core)
    halo = [permute(jnp.stack([own[j] for j in half]), x_neighbour) for half in HALVES]

    zmat, ymat = jnp.asarray(z_matrix()), jnp.asarray(y_matrix())
    kept = 2 * SEG - KEPT
    even, odd, w = call(
        first_kernel,
        [planes(kept), planes(kept), planes(SEG)],
        [2 * SEG, 2 * SEG, 2 * SEG],
        1 << 29,
        own,
        other,
        pot,
        pot_other,
        zmat,
        ymat,
    )
    even, odd = call(
        second_kernel,
        [planes(NEAR - SEG), planes(NEAR - SEG)],
        [NEAR - KEPT, NEAR - KEPT, 2 * SEG],
        1 << 28,
        even,
        odd,
        w,
        halo[0],
        pot_halo,
        zmat,
        ymat,
    )
    (filtered,) = call(
        third_kernel,
        [planes(4, SLAB)],
        [2 * SEG, 2 * SEG, 2 * SEG],
        1 << 28,
        even,
        odd,
        w,
        halo[1],
        pot_halo,
        zmat,
        ymat,
    )

    result = jnp.zeros(orbitals.shape, F32)
    mine = ((y % 2) ^ (y // 2) ^ core) * 2 + hi
    for r in range(4):

        def to_owner(x, y, z, c):
            slab = r ^ (((y % 2) ^ (y // 2) ^ c) * 2 + z // 2)
            return (x, 2 * c + (slab >> 1), 2 * (slab & 1) + 1 - z % 2, y // 2)

        piece = permute(filtered[r], to_owner)
        result = lax.dynamic_update_slice_in_dim(result, piece[None], r ^ mine, 0)
    return result


def solution(mesh):
    return jax.shard_map(
        local,
        mesh=mesh,
        in_specs=(P("band", "space", None, None), P("space", None, None), P()),
        out_specs=P("band", "space", None, None),
        check_vma=False,
    )
```

```python
import jax
import jax.numpy as jnp
import ml_dtypes
import numpy as np
from jax import lax
from jax.experimental import pallas as pl
from jax.experimental.pallas import tpu as pltpu
from jax.sharding import PartitionSpec as P


NY, NZ = 32, 128
DEGREE = 8
RADIUS = 6
SLAB = 12
RUN = 3
SEG = 48
COEFS = (
    -5369.0 / 1800.0,
    12.0 / 7.0,
    -15.0 / 56.0,
    10.0 / 189.0,
    -1.0 / 112.0,
    2.0 / 1925.0,
    -1.0 / 16632.0,
)
CENTER = 6.75
HALF_WIDTH = 6.25
GAINS = tuple(-c / HALF_WIDTH for c in COEFS)
POT_SCALE = 2.0 / HALF_WIDTH
OUTER = (5, 6)
BF16, F32 = jnp.bfloat16, jnp.float32
AXES = ("band", "space")
VMEM_LIMIT = 16 * 1024 * 1024


def split_gain(j):
    high = np.float32(GAINS[j]).astype(ml_dtypes.bfloat16)
    low = np.float32(GAINS[j] - float(high)).astype(ml_dtypes.bfloat16)
    return high, low


def circulant(n):
    high = np.zeros((n, n), ml_dtypes.bfloat16)
    low = np.zeros((n, n), ml_dtypes.bfloat16)
    for j in range(1, RADIUS + 1):
        for i in range(n):
            for k in ((i + j) % n, (i - j) % n):
                high[i, k], low[i, k] = split_gain(j)
    return high, low


GAIN_GAP = 4.0 * sum(
    GAINS[j] - float(split_gain(j)[0]) - float(split_gain(j)[1]) for j in range(1, RADIUS + 1)
) + 2.0 * sum(GAINS[j] - float(split_gain(j)[0]) for j in OUTER)
POT_SHIFT = (-2.0 * CENTER - 3.0 * COEFS[0]) / HALF_WIDTH + GAIN_GAP


def z_matrix():
    high, low = circulant(NZ)
    return np.block([[high, low], [high, np.zeros_like(low)]])


def y_matrix():
    high, low = circulant(NY)
    outer = [np.eye(NY).astype(ml_dtypes.bfloat16) * split_gain(j)[0] for j in OUTER for _ in range(2)]
    return np.concatenate([high, high, low, *outer], axis=1)


def index_of(x, y, z, core):
    return ((z % 2) * 2 + core) * 32 + (x % 4) * 8 + y * 2 + z // 2


DEVICES = [(x, y, z, c) for x in range(4) for y in range(4) for z in range(4) for c in range(2)]


def permute(array, target):
    pairs = []
    for device in DEVICES:
        to = target(*device)
        if to is not None:
            pairs.append((index_of(*device), index_of(*to)))
    return lax.ppermute(array, AXES, pairs)


def other_core(x, y, z, core):
    return (x, y, z, 1 - core)


def x_neighbour(x, y, z, core):
    return (x - 1, y, z, 1) if core == 0 else (x + 1, y, z, 0)


def host_of(c):
    lo, core, i = c >> 3, (c >> 2) & 1, c & 3
    return core * 2 + (i >> 1), 2 * (i & 1) + 1 - lo


HOSTS = [host_of(c) for c in range(16)]


def low_slab(y, core):
    return (y // 2) ^ (y % 2) ^ core


def source_of_run(core):
    runs = [low_slab(y, core) * 8 + (z // 2) * 4 + (y // 2) * 2 + z % 2 for y, z in HOSTS]
    return [runs.index(run) for run in range(16)]


HALVES = [[j for j, (y, z) in enumerate(HOSTS) if low_slab(y, 0) == far] for far in range(2)]


def place():
    band, space = lax.axis_index("band"), lax.axis_index("space")
    return band // 2, band % 2, (space // 2) % 4, space % 2


def mix_kernel(rotation, first, second, third, fourth, out):
    lo, core, y, hi = place()
    for c in range(0, 16, 2):
        totals = [None, None]
        for r, ref in enumerate((first, second, third, fourth)):
            band = 2 * (lo ^ (r & 1)) + ((r >> 1) ^ (y // 2) ^ core)
            for i in range(4):
                cells = ref[i]
                for d in range(2):
                    term = rotation[4 * band + i, c + d] * cells
                    totals[d] = term if totals[d] is None else totals[d] + term
        for d in range(2):
            out[c + d] = totals[d]


def block(a, b, w, w_at, zmat, ymat, at, first):
    n = SLAB
    u = a[at : at + n]
    wide = a[at - RADIUS : at + n + RADIUS].astype(BF16)
    high = wide[RADIUS : RADIUS + n]
    low = (u - high.astype(F32)).astype(BF16)
    both = jnp.concatenate([high.reshape(n * NY, NZ), low.reshape(n * NY, NZ)], axis=1)
    zz = jnp.dot(both, zmat[...], preferred_element_type=F32)
    z = (zz[:, :NZ] + zz[:, NZ:]).reshape(n, NY, NZ)
    ys = []
    for i in range(0, n, 2):
        rows = [jnp.concatenate([q[i], q[i + 1]], axis=1) for q in (high, low, high)]
        for j in OUTER:
            for q in (RADIUS + i + j, RADIUS + i - j):
                rows.append(jnp.concatenate([wide[q], wide[q + 1]], axis=1))
        pair = jnp.dot(ymat[...], jnp.concatenate(rows, axis=0), preferred_element_type=F32)
        ys += [pair[:, :NZ], pair[:, NZ:]]
    for r in range(0, NY, 8):
        x = a[at - RADIUS : at + n + RADIUS, r : r + 8]
        total = w[at - w_at : at - w_at + n, r : r + 8] * x[RADIUS : RADIUS + n] + z[:, r : r + 8]
        total = total + jnp.stack([t[r : r + 8] for t in ys])
        for j in range(1, OUTER[0]):
            near = x[RADIUS + j : RADIUS + j + n] + x[RADIUS - j : RADIUS - j + n]
            total = total + GAINS[j] * near
        if first:
            b[at : at + n, r : r + 8] = 0.5 * total
        else:
            b[at : at + n, r : r + 8] = total - b[at : at + n, r : r + 8]


KEPT = SEG - RADIUS


def lay_segment(ref, to, at, core, same):
    ahead = source_of_run(1 if same else 0)
    back = source_of_run(0 if same else 1)
    for s in range(16):
        source = jnp.where(core == 1, ahead[s], back[15 - s])
        for t in range(RUN):
            to[at + RUN * s + t] = ref[source, jnp.where(core == 1, t, RUN - 1 - t)]


def lay_potential(ref, to, at, core, core_from, y, hi, slabs=4):
    for s in range(slabs):
        slab = jnp.where(core == 1, s, 3 - s)
        source = ((slab & 1) ^ hi) * 2 + ((slab >> 1) ^ low_slab(y, core_from))
        for t in range(SLAB):
            plane = ref[source, jnp.where(core == 1, t, SLAB - 1 - t)]
            to[at + SLAB * s + t] = plane * POT_SCALE + POT_SHIFT


def first_kernel(own, other, pot, pot_other, zmat, ymat, even_out, odd_out, w_out, even, odd, w):
    lo, core, y, hi = place()
    lay_segment(other, even, 0, core, False)
    lay_segment(own, even, SEG, core, True)
    lay_potential(pot_other, w, 0, core, 1 - core, y, hi)
    lay_potential(pot, w, SEG, core, core, y, hi)
    for k in range(1, DEGREE):
        a, b = (even, odd) if k % 2 else (odd, even)
        for at in range(RADIUS * k, 2 * SEG - RADIUS * k, SLAB):
            block(a, b, w, 0, zmat, ymat, at, k == 1)
    even_out[...] = even[KEPT:]
    odd_out[...] = odd[KEPT:]
    w_out[...] = w[SEG:]


def lay_half(ref, to, at, core, half):
    ahead, back = source_of_run(0), source_of_run(1)
    for s in range(8):
        slots = [HALVES[half].index(table) for table in (ahead[8 * half + s], back[15 - 8 * half - s])]
        source = jnp.where(core == 1, *slots)
        for t in range(RUN):
            to[at + RUN * s + t] = ref[source, jnp.where(core == 1, t, RUN - 1 - t)]


NEAR = 3 * SEG - SEG // 2


def second_kernel(even_in, odd_in, w_in, halo, pot, zmat, ymat, even_out, odd_out, even, odd, w):
    lo, core, y, hi = place()
    shift = KEPT
    even[0 : 2 * SEG - shift] = even_in[...]
    odd[0 : 2 * SEG - shift] = odd_in[...]
    w[0:SEG] = w_in[...]
    lay_half(halo, even, 2 * SEG - shift, core, 0)
    lay_potential(pot, w, SEG, core, 1 - core, y, hi, 2)
    for k in range(1, DEGREE + 1):
        a, b = (even, odd) if k % 2 else (odd, even)
        for at in range(2 * SEG - RADIUS * k, NEAR - RADIUS * k, SLAB):
            block(a, b, w, SEG - shift, zmat, ymat, at - shift, k == 1)
    even_out[...] = even[RADIUS:]
    odd_out[...] = odd[RADIUS:]


def third_kernel(even_in, odd_in, w_in, halo, pot, zmat, ymat, out, even, odd, w):
    lo, core, y, hi = place()
    shift = SEG
    even[0 : NEAR - shift] = even_in[...]
    odd[0 : NEAR - shift] = odd_in[...]
    w[SEG // 2 : SEG] = w_in[SEG // 2 :]
    lay_half(halo, even, NEAR - shift, core, 1)
    lay_potential(pot, w, SEG, core, 1 - core, y, hi)
    for k in range(1, DEGREE + 1):
        a, b = (even, odd) if k % 2 else (odd, even)
        for at in range(NEAR - RADIUS * k, 3 * SEG - RADIUS * k, SLAB):
            block(a, b, w, SEG - shift, zmat, ymat, at - shift, k == 1)
    mine = ((y % 2) ^ (y // 2) ^ core) * 2 + hi
    for s in range(4):
        slot = jnp.where(core == 1, s, 3 - s) ^ mine
        for t in range(SLAB):
            plane = even[SEG - shift + SLAB * s + t]
            out[slot, jnp.where(core == 1, t, SLAB - 1 - t)] = plane


def planes(*lead):
    return jax.ShapeDtypeStruct((*lead, NY, NZ), F32)


def vmem(n):
    return [pl.BlockSpec(memory_space=pltpu.VMEM)] * n


def call(kernel, outs, scratch, flops, *operands, scalars=0):
    specs = [pl.BlockSpec(memory_space=pltpu.SMEM)] * scalars + vmem(len(operands) - scalars)
    moved = 4 * sum(x.size for x in (*operands, *outs))
    return pl.pallas_call(
        kernel,
        out_shape=outs,
        in_specs=specs,
        out_specs=vmem(len(outs)),
        scratch_shapes=[pltpu.VMEM((n, NY, NZ), F32) for n in scratch],
        compiler_params=pltpu.CompilerParams(vmem_limit_bytes=VMEM_LIMIT),
        cost_estimate=pl.CostEstimate(flops=flops, bytes_accessed=moved, transcendentals=0),
    )(*operands)


def spread_run(cells, r):
    def to_run(x, y, z, c):
        far, core = (r >> 1) ^ c ^ (y // 2), y // 2
        return (x, y if far == core else 3 - y, z ^ (r & 1), core)

    return permute(cells, to_run)


def local(orbitals, potential, rotation):
    lo, core, y, hi = place()
    runs = [2 * ((r >> 1) ^ core ^ (y // 2)) + (lo ^ (r & 1)) for r in range(4)]
    cells = [lax.dynamic_slice_in_dim(orbitals, RUN * run, RUN, 1) for run in runs]
    near = permute(potential, lambda x, y, z, c: (x, 3 - y, z, c) if c == y // 2 else None)
    far = permute(potential, lambda x, y, z, c: (x, y ^ 1 if c == y // 2 else y ^ 2, z, y // 2))
    near, *cells = lax.optimization_barrier((near, *cells))
    near = jnp.where(core == y // 2, potential, near)
    pair = jnp.stack([near, far])
    next_z = permute(pair, lambda x, y, z, c: (x, y, 3 - z, c))
    pot = jnp.concatenate([pair, next_z])
    groups = [spread_run(part, r) for r, part in enumerate(cells)]
    (mixed,) = call(mix_kernel, [planes(16, RUN)], [], 1 << 22, rotation, *groups, scalars=1)
    pot_halo = permute(pot, x_neighbour)
    pot_other = permute(pot, other_core)
    plane_of_hosts = [[index_of(x, *chip, c) for chip in HOSTS] for x in range(4) for c in range(2)]
    own = lax.all_to_all(mixed, AXES, 0, 0, tiled=True, axis_index_groups=plane_of_hosts)
    own, pot_halo, pot_other = lax.optimization_barrier((own, pot_halo, pot_other))
    other = permute(own, other_core)
    halo = [permute(jnp.stack([own[j] for j in half]), x_neighbour) for half in HALVES]

    zmat, ymat = jnp.asarray(z_matrix()), jnp.asarray(y_matrix())
    kept = 2 * SEG - KEPT
    even, odd, w = call(
        first_kernel,
        [planes(kept), planes(kept), planes(SEG)],
        [2 * SEG, 2 * SEG, 2 * SEG],
        1 << 29,
        own,
        other,
        pot,
        pot_other,
        zmat,
        ymat,
    )
    even, odd = call(
        second_kernel,
        [planes(NEAR - SEG), planes(NEAR - SEG)],
        [NEAR - KEPT, NEAR - KEPT, 2 * SEG],
        1 << 28,
        even,
        odd,
        w,
        halo[0],
        pot_halo,
        zmat,
        ymat,
    )
    (filtered,) = call(
        third_kernel,
        [planes(4, SLAB)],
        [2 * SEG, 2 * SEG, 2 * SEG],
        1 << 28,
        even,
        odd,
        w,
        halo[1],
        pot_halo,
        zmat,
        ymat,
    )

    result = jnp.zeros(orbitals.shape, F32)
    mine = ((y % 2) ^ (y // 2) ^ core) * 2 + hi
    for r in range(4):

        def to_owner(x, y, z, c):
            slab = r ^ (((y % 2) ^ (y // 2) ^ c) * 2 + z // 2)
            return (x, 2 * c + (slab >> 1), 2 * (slab & 1) + 1 - z % 2, y // 2)

        piece = permute(filtered[r], to_owner)
        result = lax.dynamic_update_slice_in_dim(result, piece[None], r ^ mine, 0)
    return result


def solution(mesh):
    return jax.shard_map(
        local,
        mesh=mesh,
        in_specs=(P("band", "space", None, None), P("space", None, None), P()),
        out_specs=P("band", "space", None, None),
        check_vma=False,
    )
```

```python
import jax
import jax.numpy as jnp
import ml_dtypes
import numpy as np
from jax import lax
from jax.experimental import pallas as pl
from jax.experimental.pallas import tpu as pltpu
from jax.sharding import PartitionSpec as P


NY, NZ = 32, 128
DEGREE = 8
RADIUS = 6
SLAB = 12
RUN = 3
SEG = 48
COEFS = (
    -5369.0 / 1800.0,
    12.0 / 7.0,
    -15.0 / 56.0,
    10.0 / 189.0,
    -1.0 / 112.0,
    2.0 / 1925.0,
    -1.0 / 16632.0,
)
CENTER = 6.75
HALF_WIDTH = 6.25
GAINS = tuple(-c / HALF_WIDTH for c in COEFS)
POT_SCALE = 2.0 / HALF_WIDTH
OUTER = (5, 6)
BF16, F32 = jnp.bfloat16, jnp.float32
AXES = ("band", "space")
VMEM_LIMIT = 16 * 1024 * 1024


def split_gain(j):
    high = np.float32(GAINS[j]).astype(ml_dtypes.bfloat16)
    low = np.float32(GAINS[j] - float(high)).astype(ml_dtypes.bfloat16)
    return high, low


def circulant(n):
    high = np.zeros((n, n), ml_dtypes.bfloat16)
    low = np.zeros((n, n), ml_dtypes.bfloat16)
    for j in range(1, RADIUS + 1):
        for i in range(n):
            for k in ((i + j) % n, (i - j) % n):
                high[i, k], low[i, k] = split_gain(j)
    return high, low


GAIN_GAP = 4.0 * sum(
    GAINS[j] - float(split_gain(j)[0]) - float(split_gain(j)[1]) for j in range(1, RADIUS + 1)
) + 2.0 * sum(GAINS[j] - float(split_gain(j)[0]) for j in OUTER)
POT_SHIFT = (-2.0 * CENTER - 3.0 * COEFS[0]) / HALF_WIDTH + GAIN_GAP


def z_matrix():
    high, low = circulant(NZ)
    return np.block([[high, low], [high, np.zeros_like(low)]])


def y_matrix():
    high, low = circulant(NY)
    outer = [np.eye(NY).astype(ml_dtypes.bfloat16) * split_gain(j)[0] for j in OUTER for _ in range(2)]
    return np.concatenate([high, high, low, *outer], axis=1)


def index_of(x, y, z, core):
    return ((z % 2) * 2 + core) * 32 + (x % 4) * 8 + y * 2 + z // 2


DEVICES = [(x, y, z, c) for x in range(4) for y in range(4) for z in range(4) for c in range(2)]


def permute(array, target):
    pairs = []
    for device in DEVICES:
        to = target(*device)
        if to is not None:
            pairs.append((index_of(*device), index_of(*to)))
    return lax.ppermute(array, AXES, pairs)


def other_core(x, y, z, core):
    return (x, y, z, 1 - core)


def x_neighbour(x, y, z, core):
    return (x - 1, y, z, 1) if core == 0 else (x + 1, y, z, 0)


def host_of(c):
    lo, core, i = c >> 3, (c >> 2) & 1, c & 3
    return core * 2 + (i >> 1), 2 * (i & 1) + 1 - lo


HOSTS = [host_of(c) for c in range(16)]


def low_slab(y, core):
    return (y // 2) ^ (y % 2) ^ core


def source_of_run(core):
    runs = [low_slab(y, core) * 8 + (z // 2) * 4 + (y // 2) * 2 + z % 2 for y, z in HOSTS]
    return [runs.index(run) for run in range(16)]


HALVES = [[j for j, (y, z) in enumerate(HOSTS) if low_slab(y, 0) == far] for far in range(2)]


def place():
    band, space = lax.axis_index("band"), lax.axis_index("space")
    return band // 2, band % 2, (space // 2) % 4, space % 2


def mix(rotation, parts, out, start):
    lo, core, y, hi = place()
    for c in range(0, 16, 2):
        totals = [None, None] if start is None else [start[c], start[c + 1]]
        for r, ref in parts:
            band = 2 * (lo ^ (r & 1)) + ((r >> 1) ^ (y // 2) ^ core)
            for i in range(4):
                cells = ref[i]
                for d in range(2):
                    term = rotation[4 * band + i, c + d] * cells
                    totals[d] = term if totals[d] is None else totals[d] + term
        for d in range(2):
            out[c + d] = totals[d]


def mix_kernel(rotation, first, second, third, out):
    mix(rotation, ((0, first), (1, second), (2, third)), out, None)


def mix_last_kernel(rotation, fourth, sums, out):
    mix(rotation, ((3, fourth),), out, sums)


def block(a, b, w, w_at, zmat, ymat, at, first):
    n = SLAB
    u = a[at : at + n]
    wide = a[at - RADIUS : at + n + RADIUS].astype(BF16)
    high = wide[RADIUS : RADIUS + n]
    low = (u - high.astype(F32)).astype(BF16)
    both = jnp.concatenate([high.reshape(n * NY, NZ), low.reshape(n * NY, NZ)], axis=1)
    zz = jnp.dot(both, zmat[...], preferred_element_type=F32)
    z = (zz[:, :NZ] + zz[:, NZ:]).reshape(n, NY, NZ)
    ys = []
    for i in range(0, n, 2):
        rows = [jnp.concatenate([q[i], q[i + 1]], axis=1) for q in (high, low, high)]
        for j in OUTER:
            for q in (RADIUS + i + j, RADIUS + i - j):
                rows.append(jnp.concatenate([wide[q], wide[q + 1]], axis=1))
        pair = jnp.dot(ymat[...], jnp.concatenate(rows, axis=0), preferred_element_type=F32)
        ys += [pair[:, :NZ], pair[:, NZ:]]
    for r in range(0, NY, 8):
        x = a[at - RADIUS : at + n + RADIUS, r : r + 8]
        total = w[at - w_at : at - w_at + n, r : r + 8] * x[RADIUS : RADIUS + n] + z[:, r : r + 8]
        total = total + jnp.stack([t[r : r + 8] for t in ys])
        for j in range(1, OUTER[0]):
            near = x[RADIUS + j : RADIUS + j + n] + x[RADIUS - j : RADIUS - j + n]
            total = total + GAINS[j] * near
        if first:
            b[at : at + n, r : r + 8] = 0.5 * total
        else:
            b[at : at + n, r : r + 8] = total - b[at : at + n, r : r + 8]


KEPT = SEG - RADIUS


def lay_segment(ref, to, at, core, same):
    ahead = source_of_run(1 if same else 0)
    back = source_of_run(0 if same else 1)
    for s in range(16):
        source = jnp.where(core == 1, ahead[s], back[15 - s])
        for t in range(RUN):
            to[at + RUN * s + t] = ref[source, jnp.where(core == 1, t, RUN - 1 - t)]


def lay_potential(ref, to, at, core, core_from, y, hi, slabs=4):
    for s in range(slabs):
        slab = jnp.where(core == 1, s, 3 - s)
        source = ((slab & 1) ^ hi) * 2 + ((slab >> 1) ^ low_slab(y, core_from))
        for t in range(SLAB):
            plane = ref[source, jnp.where(core == 1, t, SLAB - 1 - t)]
            to[at + SLAB * s + t] = plane * POT_SCALE + POT_SHIFT


def first_kernel(own, other, pot, pot_other, zmat, ymat, even_out, odd_out, w_out, even, odd, w):
    lo, core, y, hi = place()
    lay_segment(other, even, 0, core, False)
    lay_segment(own, even, SEG, core, True)
    lay_potential(pot_other, w, 0, core, 1 - core, y, hi)
    lay_potential(pot, w, SEG, core, core, y, hi)
    for k in range(1, DEGREE):
        a, b = (even, odd) if k % 2 else (odd, even)
        for at in range(RADIUS * k, 2 * SEG - RADIUS * k, SLAB):
            block(a, b, w, 0, zmat, ymat, at, k == 1)
    even_out[...] = even[KEPT:]
    odd_out[...] = odd[KEPT:]
    w_out[...] = w[SEG:]


def lay_half(ref, to, at, core, half):
    ahead, back = source_of_run(0), source_of_run(1)
    for s in range(8):
        slots = [HALVES[half].index(table) for table in (ahead[8 * half + s], back[15 - 8 * half - s])]
        source = jnp.where(core == 1, *slots)
        for t in range(RUN):
            to[at + RUN * s + t] = ref[source, jnp.where(core == 1, t, RUN - 1 - t)]


NEAR = 3 * SEG - SEG // 2


def second_kernel(even_in, odd_in, w_in, halo, pot, zmat, ymat, even_out, odd_out, even, odd, w):
    lo, core, y, hi = place()
    shift = KEPT
    even[0 : 2 * SEG - shift] = even_in[...]
    odd[0 : 2 * SEG - shift] = odd_in[...]
    w[0:SEG] = w_in[...]
    lay_half(halo, even, 2 * SEG - shift, core, 0)
    lay_potential(pot, w, SEG, core, 1 - core, y, hi, 2)
    for k in range(1, DEGREE + 1):
        a, b = (even, odd) if k % 2 else (odd, even)
        for at in range(2 * SEG - RADIUS * k, NEAR - RADIUS * k, SLAB):
            block(a, b, w, SEG - shift, zmat, ymat, at - shift, k == 1)
    even_out[...] = even[RADIUS:]
    odd_out[...] = odd[RADIUS:]


def third_kernel(even_in, odd_in, w_in, halo, pot, zmat, ymat, out, even, odd, w):
    lo, core, y, hi = place()
    shift = SEG
    even[0 : NEAR - shift] = even_in[...]
    odd[0 : NEAR - shift] = odd_in[...]
    w[SEG // 2 : SEG] = w_in[SEG // 2 :]
    lay_half(halo, even, NEAR - shift, core, 1)
    lay_potential(pot, w, SEG, core, 1 - core, y, hi)
    for k in range(1, DEGREE + 1):
        a, b = (even, odd) if k % 2 else (odd, even)
        for at in range(NEAR - RADIUS * k, 3 * SEG - RADIUS * k, SLAB):
            block(a, b, w, SEG - shift, zmat, ymat, at - shift, k == 1)
    mine = ((y % 2) ^ (y // 2) ^ core) * 2 + hi
    for s in range(4):
        slot = jnp.where(core == 1, s, 3 - s) ^ mine
        for t in range(SLAB):
            plane = even[SEG - shift + SLAB * s + t]
            out[slot, jnp.where(core == 1, t, SLAB - 1 - t)] = plane


def planes(*lead):
    return jax.ShapeDtypeStruct((*lead, NY, NZ), F32)


def vmem(n):
    return [pl.BlockSpec(memory_space=pltpu.VMEM)] * n


def call(kernel, outs, scratch, flops, *operands, scalars=0):
    specs = [pl.BlockSpec(memory_space=pltpu.SMEM)] * scalars + vmem(len(operands) - scalars)
    moved = 4 * sum(x.size for x in (*operands, *outs))
    return pl.pallas_call(
        kernel,
        out_shape=outs,
        in_specs=specs,
        out_specs=vmem(len(outs)),
        scratch_shapes=[pltpu.VMEM((n, NY, NZ), F32) for n in scratch],
        compiler_params=pltpu.CompilerParams(vmem_limit_bytes=VMEM_LIMIT),
        cost_estimate=pl.CostEstimate(flops=flops, bytes_accessed=moved, transcendentals=0),
    )(*operands)


def spread_run(cells, r):
    def to_run(x, y, z, c):
        far, core = (r >> 1) ^ c ^ (y // 2), y // 2
        return (x, y if far == core else 3 - y, z ^ (r & 1), core)

    return permute(cells, to_run)


def local(orbitals, potential, rotation):
    lo, core, y, hi = place()
    runs = [2 * ((r >> 1) ^ core ^ (y // 2)) + (lo ^ (r & 1)) for r in range(4)]
    cells = [lax.dynamic_slice_in_dim(orbitals, RUN * run, RUN, 1) for run in runs]
    near = permute(potential, lambda x, y, z, c: (x, 3 - y, z, c) if c == y // 2 else None)
    far = permute(potential, lambda x, y, z, c: (x, y ^ 1 if c == y // 2 else y ^ 2, z, y // 2))
    near, *cells = lax.optimization_barrier((near, *cells))
    near = jnp.where(core == y // 2, potential, near)
    pair = jnp.stack([near, far])
    next_z = permute(pair, lambda x, y, z, c: (x, y, 3 - z, c))
    pot = jnp.concatenate([pair, next_z])
    groups = [spread_run(part, r) for r, part in enumerate(cells)]
    (sums,) = call(mix_kernel, [planes(16, RUN)], [], 3 << 20, rotation, *groups[:3], scalars=1)
    (mixed,) = call(mix_last_kernel, [planes(16, RUN)], [], 1 << 20, rotation, groups[3], sums, scalars=1)
    pot_halo = permute(pot, x_neighbour)
    pot_other = permute(pot, other_core)
    plane_of_hosts = [[index_of(x, *chip, c) for chip in HOSTS] for x in range(4) for c in range(2)]
    own = lax.all_to_all(mixed, AXES, 0, 0, tiled=True, axis_index_groups=plane_of_hosts)
    own, pot_halo, pot_other = lax.optimization_barrier((own, pot_halo, pot_other))
    other = permute(own, other_core)
    halo = [permute(jnp.stack([own[j] for j in half]), x_neighbour) for half in HALVES]

    zmat, ymat = jnp.asarray(z_matrix()), jnp.asarray(y_matrix())
    kept = 2 * SEG - KEPT
    even, odd, w = call(
        first_kernel,
        [planes(kept), planes(kept), planes(SEG)],
        [2 * SEG, 2 * SEG, 2 * SEG],
        1 << 29,
        own,
        other,
        pot,
        pot_other,
        zmat,
        ymat,
    )
    even, odd = call(
        second_kernel,
        [planes(NEAR - SEG), planes(NEAR - SEG)],
        [NEAR - KEPT, NEAR - KEPT, 2 * SEG],
        1 << 28,
        even,
        odd,
        w,
        halo[0],
        pot_halo,
        zmat,
        ymat,
    )
    (filtered,) = call(
        third_kernel,
        [planes(4, SLAB)],
        [2 * SEG, 2 * SEG, 2 * SEG],
        1 << 28,
        even,
        odd,
        w,
        halo[1],
        pot_halo,
        zmat,
        ymat,
    )

    result = jnp.zeros(orbitals.shape, F32)
    mine = ((y % 2) ^ (y // 2) ^ core) * 2 + hi
    for r in range(4):

        def to_owner(x, y, z, c):
            slab = r ^ (((y % 2) ^ (y // 2) ^ c) * 2 + z // 2)
            return (x, 2 * c + (slab >> 1), 2 * (slab & 1) + 1 - z % 2, y // 2)

        piece = permute(filtered[r], to_owner)
        result = lax.dynamic_update_slice_in_dim(result, piece[None], r ^ mine, 0)
    return result


def solution(mesh):
    return jax.shard_map(
        local,
        mesh=mesh,
        in_specs=(P("band", "space", None, None), P("space", None, None), P()),
        out_specs=P("band", "space", None, None),
        check_vma=False,
    )
```

```python
import jax
import jax.numpy as jnp
import ml_dtypes
import numpy as np
from jax import lax
from jax.experimental import pallas as pl
from jax.experimental.pallas import tpu as pltpu
from jax.sharding import PartitionSpec as P


NY, NZ = 32, 128
DEGREE = 8
RADIUS = 6
SLAB = 12
RUN = 3
SEG = 48
COEFS = (
    -5369.0 / 1800.0,
    12.0 / 7.0,
    -15.0 / 56.0,
    10.0 / 189.0,
    -1.0 / 112.0,
    2.0 / 1925.0,
    -1.0 / 16632.0,
)
CENTER = 6.75
HALF_WIDTH = 6.25
GAINS = tuple(-c / HALF_WIDTH for c in COEFS)
POT_SCALE = 2.0 / HALF_WIDTH
OUTER = (5, 6)
BF16, F32 = jnp.bfloat16, jnp.float32
AXES = ("band", "space")
VMEM_LIMIT = 16 * 1024 * 1024


def split_gain(j):
    high = np.float32(GAINS[j]).astype(ml_dtypes.bfloat16)
    low = np.float32(GAINS[j] - float(high)).astype(ml_dtypes.bfloat16)
    return high, low


def circulant(n):
    high = np.zeros((n, n), ml_dtypes.bfloat16)
    low = np.zeros((n, n), ml_dtypes.bfloat16)
    for j in range(1, RADIUS + 1):
        for i in range(n):
            for k in ((i + j) % n, (i - j) % n):
                high[i, k], low[i, k] = split_gain(j)
    return high, low


GAIN_GAP = 4.0 * sum(
    GAINS[j] - float(split_gain(j)[0]) - float(split_gain(j)[1]) for j in range(1, RADIUS + 1)
) + 2.0 * sum(GAINS[j] - float(split_gain(j)[0]) for j in OUTER)
POT_SHIFT = (-2.0 * CENTER - 3.0 * COEFS[0]) / HALF_WIDTH + GAIN_GAP


def z_matrix():
    high, low = circulant(NZ)
    return np.block([[high, low], [high, np.zeros_like(low)]])


def y_matrix():
    high, low = circulant(NY)
    outer = [np.eye(NY).astype(ml_dtypes.bfloat16) * split_gain(j)[0] for j in OUTER for _ in range(2)]
    return np.concatenate([high, high, low, *outer], axis=1)


def index_of(x, y, z, core):
    return ((z % 2) * 2 + core) * 32 + (x % 4) * 8 + y * 2 + z // 2


DEVICES = [(x, y, z, c) for x in range(4) for y in range(4) for z in range(4) for c in range(2)]


def permute(array, target):
    pairs = []
    for device in DEVICES:
        to = target(*device)
        if to is not None:
            pairs.append((index_of(*device), index_of(*to)))
    return lax.ppermute(array, AXES, pairs)


def other_core(x, y, z, core):
    return (x, y, z, 1 - core)


def x_neighbour(x, y, z, core):
    return (x - 1, y, z, 1) if core == 0 else (x + 1, y, z, 0)


def host_of(c):
    lo, core, i = c >> 3, (c >> 2) & 1, c & 3
    return core * 2 + (i >> 1), 2 * (i & 1) + 1 - lo


HOSTS = [host_of(c) for c in range(16)]


def low_slab(y, core):
    return (y // 2) ^ (y % 2) ^ core


def source_of_run(core):
    runs = [low_slab(y, core) * 8 + (z // 2) * 4 + (y // 2) * 2 + z % 2 for y, z in HOSTS]
    return [runs.index(run) for run in range(16)]


HALVES = [[j for j, (y, z) in enumerate(HOSTS) if low_slab(y, 0) == far] for far in range(2)]


def place():
    band, space = lax.axis_index("band"), lax.axis_index("space")
    return band // 2, band % 2, (space // 2) % 4, space % 2


def mix(rotation, parts, out, start):
    lo, core, y, hi = place()
    for c in range(0, 16, 2):
        totals = [None, None] if start is None else [start[c], start[c + 1]]
        for r, ref in parts:
            band = 2 * (lo ^ (r & 1)) + ((r >> 1) ^ (y // 2) ^ core)
            for i in range(4):
                cells = ref[i]
                for d in range(2):
                    term = rotation[4 * band + i, c + d] * cells
                    totals[d] = term if totals[d] is None else totals[d] + term
        for d in range(2):
            out[c + d] = totals[d]


def mix_kernel(rotation, first, second, third, out):
    mix(rotation, ((1, first), (3, second), (2, third)), out, None)


def mix_last_kernel(rotation, fourth, sums, out):
    mix(rotation, ((0, fourth),), out, sums)


def block(a, b, w, w_at, zmat, ymat, at, first):
    n = SLAB
    u = a[at : at + n]
    wide = a[at - RADIUS : at + n + RADIUS].astype(BF16)
    high = wide[RADIUS : RADIUS + n]
    low = (u - high.astype(F32)).astype(BF16)
    both = jnp.concatenate([high.reshape(n * NY, NZ), low.reshape(n * NY, NZ)], axis=1)
    zz = jnp.dot(both, zmat[...], preferred_element_type=F32)
    z = (zz[:, :NZ] + zz[:, NZ:]).reshape(n, NY, NZ)
    ys = []
    for i in range(0, n, 2):
        rows = [jnp.concatenate([q[i], q[i + 1]], axis=1) for q in (high, low, high)]
        for j in OUTER:
            for q in (RADIUS + i + j, RADIUS + i - j):
                rows.append(jnp.concatenate([wide[q], wide[q + 1]], axis=1))
        pair = jnp.dot(ymat[...], jnp.concatenate(rows, axis=0), preferred_element_type=F32)
        ys += [pair[:, :NZ], pair[:, NZ:]]
    for r in range(0, NY, 8):
        x = a[at - RADIUS : at + n + RADIUS, r : r + 8]
        total = w[at - w_at : at - w_at + n, r : r + 8] * x[RADIUS : RADIUS + n] + z[:, r : r + 8]
        total = total + jnp.stack([t[r : r + 8] for t in ys])
        for j in range(1, OUTER[0]):
            near = x[RADIUS + j : RADIUS + j + n] + x[RADIUS - j : RADIUS - j + n]
            total = total + GAINS[j] * near
        if first:
            b[at : at + n, r : r + 8] = 0.5 * total
        else:
            b[at : at + n, r : r + 8] = total - b[at : at + n, r : r + 8]


KEPT = SEG - RADIUS


def lay_segment(ref, to, at, core, same):
    ahead = source_of_run(1 if same else 0)
    back = source_of_run(0 if same else 1)
    for s in range(16):
        source = jnp.where(core == 1, ahead[s], back[15 - s])
        for t in range(RUN):
            to[at + RUN * s + t] = ref[source, jnp.where(core == 1, t, RUN - 1 - t)]


def lay_potential(ref, to, at, core, core_from, y, hi, slabs=4):
    for s in range(slabs):
        slab = jnp.where(core == 1, s, 3 - s)
        source = ((slab & 1) ^ hi) * 2 + ((slab >> 1) ^ low_slab(y, core_from))
        for t in range(SLAB):
            plane = ref[source, jnp.where(core == 1, t, SLAB - 1 - t)]
            to[at + SLAB * s + t] = plane * POT_SCALE + POT_SHIFT


def first_kernel(own, other, pot, pot_other, zmat, ymat, even_out, odd_out, w_out, even, odd, w):
    lo, core, y, hi = place()
    lay_segment(other, even, 0, core, False)
    lay_segment(own, even, SEG, core, True)
    lay_potential(pot_other, w, 0, core, 1 - core, y, hi)
    lay_potential(pot, w, SEG, core, core, y, hi)
    for k in range(1, DEGREE):
        a, b = (even, odd) if k % 2 else (odd, even)
        for at in range(RADIUS * k, 2 * SEG - RADIUS * k, SLAB):
            block(a, b, w, 0, zmat, ymat, at, k == 1)
    even_out[...] = even[KEPT:]
    odd_out[...] = odd[KEPT:]
    w_out[...] = w[SEG:]


def lay_half(ref, to, at, core, half):
    ahead, back = source_of_run(0), source_of_run(1)
    for s in range(8):
        slots = [HALVES[half].index(table) for table in (ahead[8 * half + s], back[15 - 8 * half - s])]
        source = jnp.where(core == 1, *slots)
        for t in range(RUN):
            to[at + RUN * s + t] = ref[source, jnp.where(core == 1, t, RUN - 1 - t)]


NEAR = 3 * SEG - SEG // 2


def second_kernel(even_in, odd_in, w_in, halo, pot, zmat, ymat, even_out, odd_out, even, odd, w):
    lo, core, y, hi = place()
    shift = KEPT
    even[0 : 2 * SEG - shift] = even_in[...]
    odd[0 : 2 * SEG - shift] = odd_in[...]
    w[0:SEG] = w_in[...]
    lay_half(halo, even, 2 * SEG - shift, core, 0)
    lay_potential(pot, w, SEG, core, 1 - core, y, hi, 2)
    for k in range(1, DEGREE + 1):
        a, b = (even, odd) if k % 2 else (odd, even)
        for at in range(2 * SEG - RADIUS * k, NEAR - RADIUS * k, SLAB):
            block(a, b, w, SEG - shift, zmat, ymat, at - shift, k == 1)
    even_out[...] = even[RADIUS:]
    odd_out[...] = odd[RADIUS:]


def third_kernel(even_in, odd_in, w_in, halo, pot, zmat, ymat, out, even, odd, w):
    lo, core, y, hi = place()
    shift = SEG
    even[0 : NEAR - shift] = even_in[...]
    odd[0 : NEAR - shift] = odd_in[...]
    w[SEG // 2 : SEG] = w_in[SEG // 2 :]
    lay_half(halo, even, NEAR - shift, core, 1)
    lay_potential(pot, w, SEG, core, 1 - core, y, hi)
    for k in range(1, DEGREE + 1):
        a, b = (even, odd) if k % 2 else (odd, even)
        for at in range(NEAR - RADIUS * k, 3 * SEG - RADIUS * k, SLAB):
            block(a, b, w, SEG - shift, zmat, ymat, at - shift, k == 1)
    mine = ((y % 2) ^ (y // 2) ^ core) * 2 + hi
    for s in range(4):
        slot = jnp.where(core == 1, s, 3 - s) ^ mine
        for t in range(SLAB):
            plane = even[SEG - shift + SLAB * s + t]
            out[slot, jnp.where(core == 1, t, SLAB - 1 - t)] = plane


def planes(*lead):
    return jax.ShapeDtypeStruct((*lead, NY, NZ), F32)


def vmem(n):
    return [pl.BlockSpec(memory_space=pltpu.VMEM)] * n


def call(kernel, outs, scratch, flops, *operands, scalars=0):
    specs = [pl.BlockSpec(memory_space=pltpu.SMEM)] * scalars + vmem(len(operands) - scalars)
    moved = 4 * sum(x.size for x in (*operands, *outs))
    return pl.pallas_call(
        kernel,
        out_shape=outs,
        in_specs=specs,
        out_specs=vmem(len(outs)),
        scratch_shapes=[pltpu.VMEM((n, NY, NZ), F32) for n in scratch],
        compiler_params=pltpu.CompilerParams(vmem_limit_bytes=VMEM_LIMIT),
        cost_estimate=pl.CostEstimate(flops=flops, bytes_accessed=moved, transcendentals=0),
    )(*operands)


def spread_run(cells, r):
    def to_run(x, y, z, c):
        far, core = (r >> 1) ^ c ^ (y // 2), y // 2
        return (x, y if far == core else 3 - y, z ^ (r & 1), core)

    return permute(cells, to_run)


def local(orbitals, potential, rotation):
    lo, core, y, hi = place()
    runs = [2 * ((r >> 1) ^ core ^ (y // 2)) + (lo ^ (r & 1)) for r in range(4)]
    cells = [lax.dynamic_slice_in_dim(orbitals, RUN * run, RUN, 1) for run in runs]
    near = permute(potential, lambda x, y, z, c: (x, 3 - y, z, c) if c == y // 2 else None)
    far = permute(potential, lambda x, y, z, c: (x, y ^ 1 if c == y // 2 else y ^ 2, z, y // 2))
    near, *cells = lax.optimization_barrier((near, *cells))
    near = jnp.where(core == y // 2, potential, near)
    pair = jnp.stack([near, far])
    next_z = permute(pair, lambda x, y, z, c: (x, y, 3 - z, c))
    pot = jnp.concatenate([pair, next_z])
    groups = [spread_run(part, r) for r, part in enumerate(cells)]
    (sums,) = call(mix_kernel, [planes(16, RUN)], [], 3 << 20, rotation, groups[1], groups[3], groups[2], scalars=1)
    (mixed,) = call(mix_last_kernel, [planes(16, RUN)], [], 1 << 20, rotation, groups[0], sums, scalars=1)
    pot_halo = permute(pot, x_neighbour)
    pot_other = permute(pot, other_core)
    plane_of_hosts = [[index_of(x, *chip, c) for chip in HOSTS] for x in range(4) for c in range(2)]
    own = lax.all_to_all(mixed, AXES, 0, 0, tiled=True, axis_index_groups=plane_of_hosts)
    own, pot_halo, pot_other = lax.optimization_barrier((own, pot_halo, pot_other))
    other = permute(own, other_core)
    halo = [permute(jnp.stack([own[j] for j in half]), x_neighbour) for half in HALVES]

    zmat, ymat = jnp.asarray(z_matrix()), jnp.asarray(y_matrix())
    kept = 2 * SEG - KEPT
    even, odd, w = call(
        first_kernel,
        [planes(kept), planes(kept), planes(SEG)],
        [2 * SEG, 2 * SEG, 2 * SEG],
        1 << 29,
        own,
        other,
        pot,
        pot_other,
        zmat,
        ymat,
    )
    even, odd = call(
        second_kernel,
        [planes(NEAR - SEG), planes(NEAR - SEG)],
        [NEAR - KEPT, NEAR - KEPT, 2 * SEG],
        1 << 28,
        even,
        odd,
        w,
        halo[0],
        pot_halo,
        zmat,
        ymat,
    )
    (filtered,) = call(
        third_kernel,
        [planes(4, SLAB)],
        [2 * SEG, 2 * SEG, 2 * SEG],
        1 << 28,
        even,
        odd,
        w,
        halo[1],
        pot_halo,
        zmat,
        ymat,
    )

    result = jnp.zeros(orbitals.shape, F32)
    mine = ((y % 2) ^ (y // 2) ^ core) * 2 + hi
    for r in range(4):

        def to_owner(x, y, z, c):
            slab = r ^ (((y % 2) ^ (y // 2) ^ c) * 2 + z // 2)
            return (x, 2 * c + (slab >> 1), 2 * (slab & 1) + 1 - z % 2, y // 2)

        piece = permute(filtered[r], to_owner)
        result = lax.dynamic_update_slice_in_dim(result, piece[None], r ^ mine, 0)
    return result


def solution(mesh):
    return jax.shard_map(
        local,
        mesh=mesh,
        in_specs=(P("band", "space", None, None), P("space", None, None), P()),
        out_specs=P("band", "space", None, None),
        check_vma=False,
    )
```
